32 devices in a mesh: dp: 4 (over x, core), seq: 8 (over z, y).
Axes of the slice: x: 2, y: 2, z: 4, core: 2. Of those that a mesh axis runs over, the one named last changes fastest.
Arguments:
- encoded: bfloat16 [4, 1024, 2048], P('dp', 'seq'), may hold values from -6 to 6
- cotangents: bfloat16 [2, 4, 1024, 2, 2048], P(None, 'dp', 'seq'), may hold values from -6 to 6
- weights: bfloat16 [2, 2, 2048, 2048], P(None, None, None, 'dp'), may hold values from -0.125 to 0.125
Outputs:
- input_grad: bfloat16 [4, 1024, 2048], P('dp', 'seq')
- weight_grad: float32 [2048, 2, 2, 2048], P('seq', None, None, 'dp')
The draws below stay inside these ranges and needn't reach their ends.
All inputs are finite; a program needn't handle non-finite values.
Results may differ from the reference program's by a relative error of at most 0.001.
Values may be sent and summed in bfloat16 or wider, within the bound.
A program may use at most 128 MiB of HBM per device.

```python
import jax
import jax.numpy as jnp

D = 2048
E = 2048
LAYERS = 2
LENGTH = 1024
EXAMPLES = 4
TOKENS = 4096


def raised(result, key, source, target, shards_of, factor):
    def block_of(dim):
        return (jnp.arange(result.shape[dim]) // (result.shape[dim] // shards_of)).reshape((-1,) + (1,) * (result.ndim - 1 - dim))

    near = jax.random.permutation(key, shards_of)[block_of(target)]
    other_side = (block_of(target) + shards_of // 2) % shards_of
    return jnp.where((block_of(source) == near) | (block_of(source) == other_side), factor * result, result)


def levels(key, dims, cuts, smallest, top_value):
    def one(position, parts):
        heights = jax.random.uniform(jax.random.fold_in(jax.random.fold_in(key, 6), position), (parts,), jnp.float32, smallest / len(cuts), top_value / len(cuts))
        return jnp.repeat(jnp.exp(heights), dims[position] // parts).reshape((-1,) + (1,) * (len(dims) - position - 1))

    factor_of = one(*cuts[0])
    for cut in cuts[1:]:
        factor_of = factor_of * one(*cut)
    return factor_of


def normal_values(stream_key, extent, spread, reach, split=(), kind=jnp.bfloat16):
    array = spread * jax.random.normal(stream_key, extent, jnp.float32)
    if split:
        array = array * levels(stream_key, extent, split, -0.22, 0.18)
    return jnp.clip(array, -reach, reach).astype(kind)


def bell_draw_with(own_key, dims, deviation, most, shards, heavy, held_as=jnp.bfloat16):
    entries = deviation * jax.random.normal(own_key, dims, jnp.float32)
    if shards:
        entries = entries * levels(own_key, dims, shards, -0.22, 0.18)
    return jnp.clip(raised(entries, jax.random.fold_in(own_key, 3), *heavy), -most, most).astype(held_as)


def setup_inputs(seed: int = 0) -> dict:
    key_list = jax.random.split(jax.random.key(seed), 4)
    return {
        "encoded": bell_draw_with(key_list[0], (EXAMPLES, LENGTH, D), 1.0, 6.0, ((0, 4), (1, 8)), (1, 2, 8, 2.0)),
        "cotangents": bell_draw_with(key_list[1], (LAYERS, EXAMPLES, LENGTH, 2, E), 1.0, 6.0, ((1, 4), (2, 8)), (4, 1, 4, 2.0)),
        "weights": normal_values(key_list[2], (LAYERS, 2, D, E), D ** -0.5, 0.125, ((3, 4),)),
    }


def reference(encoded, cotangents, weights):
    flat_tokens = encoded.reshape(-1, encoded.shape[2])
    input_sum = jnp.zeros(flat_tokens.shape, jnp.float32)
    norm_factor = 1.0 / jnp.sqrt(jnp.float32(TOKENS))
    layer_list = []
    for layer_idx in range(LAYERS):
        part_list = []
        for part_idx in range(2):
            grad_rows = cotangents[layer_idx, :, :, part_idx, :].reshape(-1, cotangents.shape[4])
            input_sum = input_sum + jnp.dot(grad_rows, weights[layer_idx, part_idx].T, preferred_element_type=jnp.float32)
            part_list.append(jnp.dot(flat_tokens.T, grad_rows, preferred_element_type=jnp.float32) * norm_factor)
        layer_list.append(jnp.stack(part_list, axis=1))
    weight_grad = jnp.stack(layer_list, axis=1)
    input_grad = input_sum.astype(jnp.bfloat16).reshape(encoded.shape)
    return (input_grad, weight_grad)
```

```python
import jax
import jax.numpy as jnp
from jax import lax
from jax.sharding import PartitionSpec as P

F32 = jnp.float32
BF16 = jnp.bfloat16
TOP = 2.0**30


def encode(x):
    square = x * x
    return (square * x * jnp.abs(x)).astype(BF16)


def decode(y):
    y = y.astype(F32)
    root = jnp.sqrt(jnp.sqrt(jnp.abs(y)))
    return jnp.where(y < 0, -root, root)


def local(encoded, cotangents, weights):
    ndp, nseq = lax.axis_size("dp"), lax.axis_size("seq")
    nz = nseq // 2
    me, seq = lax.axis_index("dp"), lax.axis_index("seq")
    y, z = seq % 2, seq // 2
    layers, _, rows, parts, units = cotangents.shape
    feats = encoded.shape[2]
    dl = feats // nseq
    el = units // ndp
    lc = layers * parts
    tokens = rows * nseq * ndp

    def swap_dp(a, k):
        return lax.ppermute(a, "dp", [(i, i ^ k) for i in range(ndp)])

    def swap_y(a):
        return lax.ppermute(a, "seq", [(i, i ^ 1) for i in range(nseq)])

    peak = lax.pmax(
        jnp.stack([jnp.max(jnp.abs(encoded)), jnp.max(jnp.abs(cotangents))]).astype(F32),
        ("dp", "seq"),
    )
    peak = jnp.maximum(peak, 1e-30)
    inv = 1.0 / peak
    down = (peak[0] * peak[1]) * (tokens / TOP) * (1.0 / jnp.sqrt(F32(tokens)))

    blocks = cotangents[:, 0].reshape(layers, rows, parts, ndp, el)
    blocks = blocks.transpose(3, 0, 2, 1, 4).reshape(ndp, lc, rows, el)

    enc = encoded[0].reshape(rows, nz, 2, dl).transpose(2, 1, 0, 3)
    enc_own = lax.dynamic_index_in_dim(enc, y, 0, keepdims=False)
    enc_far = swap_y(lax.dynamic_index_in_dim(enc, 1 - y, 0, keepdims=False))
    enc0 = jnp.stack([enc_own, enc_far])
    enc_src = [enc0, swap_dp(enc0, 1), swap_dp(enc0, 2)]
    enc_src.append(swap_dp(enc_src[1], 2))
    enc_all = jnp.concatenate(enc_src, 0).transpose(1, 0, 2, 3).reshape(nz, 2 * ndp * rows, dl)

    near = []
    for k in range(ndp):
        b = lax.dynamic_index_in_dim(blocks, me ^ k, 0, keepdims=False)
        near.append(b if k == 0 else swap_dp(b, k))
    far = [swap_y(b) for b in near]
    cot_all = jnp.stack([jnp.stack([n, f]) for n, f in zip(near, far)])
    cot_all = cot_all.transpose(2, 0, 1, 3, 4).reshape(lc, 2 * ndp * rows, el)

    factor = inv[0] * (TOP / tokens)

    def term(b):
        e = lax.dynamic_index_in_dim(enc_all, jnp.clip(b, 0, nz - 1), 0, keepdims=False)
        t = jnp.einsum("td,cte->dce", e, cot_all, preferred_element_type=F32)
        return t * factor * inv[1]

    right = left = None
    for s in range(nz - 1):
        r = term(z + (nz - 1 - s))
        l = term(z - (nz - 1 - s))
        if s:
            r = r + decode(right)
            l = l + decode(left)
        rp, lp = [], []
        for q in range(min(s + 1, nz - 1)):
            for yy in range(2):
                rp.append((q * 2 + yy, (q + 1) * 2 + yy))
                lp.append(((nz - 1 - q) * 2 + yy, (nz - 2 - q) * 2 + yy))
        right = lax.ppermute(encode(r), "seq", rp)
        left = lax.ppermute(encode(l), "seq", lp)
    wg = term(z)
    if nz > 1:
        wg = wg + decode(right) + decode(left)
    weight_grad = (wg * down).reshape(dl, layers, parts, el)

    def part(k):
        w = weights.reshape(lc, feats, el)
        return jnp.einsum("cte,cde->td", near[k], w, preferred_element_type=F32)

    held = [part(k) for k in range(ndp)]
    bit = 1
    while bit < ndp:
        held = [
            a + b
            for a, b in zip(
                [held[k] for k in range(len(held)) if not (k & 1)],
                [swap_dp(held[k], bit) for k in range(len(held)) if k & 1],
            )
        ]
        bit *= 2
    input_grad = held[0].astype(BF16)[None]
    return (input_grad, weight_grad)


def solution(mesh):
    return jax.shard_map(
        local,
        mesh=mesh,
        in_specs=(
            P("dp", "seq", None),
            P(None, "dp", "seq", None, None),
            P(None, None, None, "dp"),
        ),
        out_specs=(P("dp", "seq", None), P("seq", None, None, "dp")),
        check_vma=False,
    )
```

```python
import jax
import jax.numpy as jnp
from jax import lax
from jax.experimental import pallas as pl
from jax.experimental.pallas import tpu as pltpu
from jax.sharding import PartitionSpec as P

F32 = jnp.float32
BF16 = jnp.bfloat16
TOP = 2.0**30
MESH = pl.DeviceIdType.MESH


def encode(x):
    square = x * x
    return (square * x * jnp.abs(x)).astype(BF16)


def decode(y):
    y = y.astype(F32)
    root = jnp.sqrt(jnp.sqrt(jnp.abs(y)))
    return jnp.where(y < 0, -root, root)


def kernel(ndp, nseq, cot, enc, w, ig, wg, near, far, encs, recv, send, wv, igs, igr, xs, xr, pks, pkr, pkz,
           wsem, ss_cot, rs_cot, ss_enc, rs_enc, ss_z, rs_z, ss_ig, rs_ig, ss_pk, rs_pk, ss_pz, rs_pz):
    nz = nseq // 2
    _, lc, rows, el = cot.shape
    dl = enc.shape[2]
    feats = w.shape[1]
    tokens = rows * nseq * ndp
    me, seq = lax.axis_index("dp"), lax.axis_index("seq")
    y, z = seq % 2, seq // 2
    pair = me + 1 - 2 * (me % 2)
    across = me + 2 - 4 * (me // 2)
    dps = (me, pair, across, 3 - me)
    ypeer = z * 2 + 1 - y

    def dp_dev(k):
        return (dps[k], seq)

    y_dev = (me, ypeer)

    def z_dev(zz):
        return (me, zz * 2 + y)

    def rcopy(src, dst, s, r, dev):
        return pltpu.make_async_remote_copy(
            src_ref=src, dst_ref=dst, send_sem=s, recv_sem=r, device_id=dev, device_id_type=MESH
        )

    barrier = pltpu.get_barrier_semaphore()
    for k in (1, 2, 3):
        pl.semaphore_signal(barrier, inc=1, device_id=dp_dev(k), device_id_type=MESH)
    pl.semaphore_signal(barrier, inc=1, device_id=y_dev, device_id_type=MESH)

    @pl.loop(1, nz)
    def _(d):
        pl.semaphore_signal(barrier, inc=1, device_id=z_dev((z + d) % nz), device_id_type=MESH)

    pl.semaphore_wait(barrier, 4 + nz - 1)

    wcopy = pltpu.make_async_copy(w, wv, wsem)

    def enc_copy(slot, src, dev):
        return rcopy(src, encs.at[slot], ss_enc.at[slot], rs_enc.at[slot], dev)

    e_y = enc_copy(1, enc.at[1 - y], y_dev)
    e_own2 = enc_copy(4, enc.at[y], dp_dev(2))
    e_own1 = enc_copy(2, enc.at[y], dp_dev(1))
    e_far2 = enc_copy(5, encs.at[1], dp_dev(2))
    e_far1 = enc_copy(3, encs.at[1], dp_dev(1))
    e_on1 = enc_copy(6, encs.at[4], dp_dev(1))
    e_on1f = enc_copy(7, encs.at[5], dp_dev(1))

    def near_ref(c, k):
        return cot.at[me, c] if k == 0 else near.at[c, k - 1]

    def dp_copy(c, k):
        return rcopy(cot.at[dps[k], c], near.at[c, k - 1], ss_cot.at[c, k], rs_cot.at[c, k], dp_dev(k))

    def y_copy(c, k):
        return rcopy(near_ref(c, k), far.at[c, k], ss_cot.at[c, 4 + k], rs_cot.at[c, 4 + k], y_dev)

    e_y.start()
    e_own2.start()
    y_copy(0, 0).start()
    dp_copy(0, 1).start()
    dp_copy(0, 2).start()
    dp_copy(0, 3).start()
    e_own1.start()
    wcopy.start()
    for c in range(1, lc):
        for k in (1, 2, 3):
            dp_copy(c, k).start()

    def cot_peak(i, m):
        return jnp.maximum(m, jnp.max(jnp.abs(cot[i // lc, i % lc].astype(F32)), axis=0, keepdims=True))

    def enc_peak(i, m):
        return jnp.maximum(m, jnp.max(jnp.abs(enc[i // nz, i % nz].astype(F32)), axis=0, keepdims=True))

    mc = jnp.max(lax.fori_loop(0, ndp * lc, cot_peak, jnp.zeros((1, el), F32)), axis=1, keepdims=True)
    me_ = jnp.max(lax.fori_loop(0, 2 * nz, enc_peak, jnp.zeros((1, rows), F32)), axis=1, keepdims=True)
    upper = lax.broadcasted_iota(jnp.int32, (8, 128), 0) < 4
    tile = jnp.where(upper, jnp.broadcast_to(me_, (8, 128)), jnp.broadcast_to(mc, (8, 128)))

    def pk_copy(i, dev):
        return rcopy(pks.at[i], pkr.at[i], ss_pk.at[i], rs_pk.at[i], dev)

    def pk_stage(i):
        pk_copy(i, None if i < 0 else (dp_dev(1), dp_dev(2), y_dev)[i]).wait_recv()
        pks[i + 1] = jnp.maximum(pks[i], pkr[i])

    pks[0] = tile
    pk_copy(0, dp_dev(1)).start()

    dp_copy(0, 1).wait_recv()
    y_copy(0, 1).start()
    pk_stage(0)
    pk_copy(1, dp_dev(2)).start()
    e_y.wait_recv()
    e_far2.start()
    e_far1.start()
    e_own2.wait_recv()
    e_on1.start()
    for k in (2, 3):
        dp_copy(0, k).wait_recv()
        y_copy(0, k).start()
    pk_stage(1)
    pk_copy(2, y_dev).start()

    def forward(c):
        for k in range(4):
            if k:
                dp_copy(c, k).wait_recv()
            y_copy(c, k).start()

    def pz_copy(d):
        return rcopy(pks.at[3], pkz.at[d], ss_pz.at[d], rs_pz.at[d], z_dev((z + d) % nz))

    e_far2.wait_recv()
    e_on1f.start()
    forward(1)
    pk_stage(2)
    pkz[0] = pks[3]

    @pl.loop(1, nz)
    def _(d):
        pz_copy(d).start()

    e_own1.wait_recv()
    e_far1.wait_recv()
    e_on1.wait_recv()
    e_on1f.wait_recv()

    @pl.loop(1, nz)
    def _(d):
        pz_copy(d).wait_recv()

    def pz_max(d, m):
        return jnp.maximum(m, pkz[d])

    peak = jnp.maximum(lax.fori_loop(1, nz, pz_max, pkz[0]), 1e-30)
    peak_e, peak_c = peak[0:1, 0:1], peak[4:5, 0:1]
    up_e = (TOP / tokens) / peak_e
    up_c = 1.0 / peak_c
    norm = 1.0 / jnp.sqrt(jnp.full((1, 1), tokens, F32))
    down = peak_e * peak_c * (tokens / TOP) * norm

    def term(b, c):
        lhs = jnp.concatenate([enc[y, b]] + [encs[s, b] for s in range(1, 2 * ndp)], axis=1)
        pieces = []
        for k in range(ndp):
            pieces += [cot[me, c] if k == 0 else near[c, k - 1], far[c, k]]
        rhs = jnp.concatenate(pieces, axis=0)
        t = jnp.dot(lhs, rhs, preferred_element_type=F32)
        return t * up_e * up_c

    lower = z < nz // 2
    way = jnp.where(lower, 0, 1)
    m = jnp.where(lower, z, nz - 1 - z)

    def z_copy(c, d, j, slot):
        return rcopy(send.at[c, slot], recv.at[c, d, j], ss_z.at[c, slot], rs_z.at[c, d, j], z_dev(z + 1 - 2 * d))

    def move(c, d, j, slot, has_prev):
        block = jnp.where(d == 0, nz - 1 - j, j)

        @pl.when(has_prev)
        def _():
            z_copy(c, d, j, slot).wait_recv()
            send[c, slot] = encode(term(block, c) + decode(recv[c, d, j]))

        @pl.when(jnp.logical_not(has_prev))
        def _():
            send[c, slot] = encode(term(block, c))

        z_copy(c, d, j, slot).start()

    def first(c):
        @pl.loop(0, nz - 1 - m)
        def _(j):
            move(c, way, j, j, m > 0)

    def second(c):
        @pl.loop(0, m)
        def _(j):
            move(c, 1 - way, j, nz - 1 - m + j, True)

    def finish(c):
        wg[c] = term(z, c)
        for d in range(2):
            j = nz - 1 - z if d == 0 else z

            @pl.when(z > 0 if d == 0 else z < nz - 1)
            def _():
                z_copy(c, d, j, 0).wait_recv()
                wg[c] = wg[c] + decode(recv[c, d, j])

        wg[c] = wg[c] * down

    step_f = 512 if feats % 512 == 0 else feats

    def partial(ka, kb, put):
        @pl.loop(0, feats // step_f)
        def _(i):
            cols = pl.ds(pl.multiple_of(i * step_f, step_f), step_f)
            acc = jnp.zeros((2 * rows, step_f), F32)
            for c in range(lc):
                lhs = jnp.concatenate([near_ref(c, ka)[...], near_ref(c, kb)[...]], axis=0)
                acc = acc + lax.dot_general(
                    lhs, wv[c, cols, :], (((1,), (1,)), ((), ())), preferred_element_type=F32
                )
            put(cols, acc)

    def ig_copy(i):
        return rcopy(igs.at[i], igr.at[i], ss_ig.at[i], rs_ig.at[i], dp_dev(1))

    x_copy = rcopy(xs.at[0], xr, ss_ig.at[2], rs_ig.at[2], dp_dev(2))

    def put_pair(cols, acc):
        igs[0, :, cols] = acc[:rows]
        igs[1, :, cols] = acc[rows:]

    def put_own(cols, acc):
        xs[0, :, cols] = acc[:rows] + igr[0, :, cols]
        xs[1, :, cols] = acc[rows:] + igr[1, :, cols]

    for c in range(lc):
        for k in range(4):
            y_copy(c, k).wait_recv()
        first(c)
        if c + 2 < lc:
            forward(c + 2)
        if c == lc - 2:
            wcopy.wait()
            partial(3, 1, put_pair)
            ig_copy(0).start()
            ig_copy(1).start()
        if c > 0:
            second(c - 1)
        if c > 1:
            finish(c - 2)
    ig_copy(0).wait_recv()
    ig_copy(1).wait_recv()
    partial(2, 0, put_own)
    x_copy.start()
    finish(lc - 2)
    second(lc - 1)
    x_copy.wait_recv()
    ig[...] = (xs[1] + xr[...]).astype(BF16)
    finish(lc - 1)

    for c in range(lc):
        for k in range(4):
            if k:
                dp_copy(c, k).wait_send()
            y_copy(c, k).wait_send()

        @pl.loop(0, nz - 1)
        def _(j):
            z_copy(c, 0, 0, j).wait_send()

    for e in (e_y, e_own1, e_own2, e_far1, e_far2, e_on1, e_on1f, ig_copy(0), ig_copy(1), x_copy):
        e.wait_send()
    for i in range(3):
        pk_copy(i, y_dev).wait_send()

    @pl.loop(1, nz)
    def _(d):
        pz_copy(d).wait_send()


def local(encoded, cotangents, weights):
    ndp, nseq = lax.axis_size("dp"), lax.axis_size("seq")
    nz = nseq // 2
    layers, _, rows, parts, units = cotangents.shape
    feats = encoded.shape[2]
    dl = feats // nseq
    el = units // ndp
    lc = layers * parts
    cot = cotangents[:, 0].reshape(layers, rows, parts, ndp, el)
    cot = cot.transpose(3, 0, 2, 1, 4).reshape(ndp, lc, rows, el)
    enc = encoded[0].reshape(rows, nz, 2, dl).transpose(2, 1, 3, 0)
    w = weights.reshape(lc, feats, el)
    dma = pltpu.SemaphoreType.DMA
    ig, wg = pl.pallas_call(
        lambda *refs: kernel(ndp, nseq, *refs),
        out_shape=(
            jax.ShapeDtypeStruct((rows, feats), BF16),
            jax.ShapeDtypeStruct((lc, dl, el), F32),
        ),
        in_specs=[
            pl.BlockSpec(memory_space=pltpu.VMEM),
            pl.BlockSpec(memory_space=pltpu.VMEM),
            pl.BlockSpec(memory_space=pl.ANY),
        ],
        out_specs=(pl.BlockSpec(memory_space=pltpu.VMEM), pl.BlockSpec(memory_space=pltpu.VMEM)),
        scratch_shapes=[
            pltpu.VMEM((lc, ndp - 1, rows, el), BF16),
            pltpu.VMEM((lc, ndp, rows, el), BF16),
            pltpu.VMEM((2 * ndp, nz, dl, rows), BF16),
            pltpu.VMEM((lc, 2, nz - 1, dl, el), BF16),
            pltpu.VMEM((lc, nz - 1, dl, el), BF16),
            pltpu.VMEM((lc, feats, el), BF16),
            pltpu.VMEM((2, rows, feats), F32),
            pltpu.VMEM((2, rows, feats), F32),
            pltpu.VMEM((2, rows, feats), F32),
            pltpu.VMEM((rows, feats), F32),
            pltpu.VMEM((4, 8, 128), F32),
            pltpu.VMEM((3, 8, 128), F32),
            pltpu.VMEM((nz, 8, 128), F32),
            dma,
            dma((lc, 8)),
            dma((lc, 8)),
            dma((8,)),
            dma((8,)),
            dma((lc, nz - 1)),
            dma((lc, 2, nz - 1)),
            dma((3,)),
            dma((3,)),
            dma((3,)),
            dma((3,)),
            dma((nz,)),
            dma((nz,)),
        ],
        compiler_params=pltpu.CompilerParams(
            collective_id=0, has_side_effects=True, vmem_limit_bytes=56 * 2**20
        ),
    )(cot, enc, w)
    weight_grad = wg.reshape(layers, parts, dl, el).transpose(2, 0, 1, 3)
    return (ig[None], weight_grad)


def solution(mesh):
    return jax.shard_map(
        local,
        mesh=mesh,
        in_specs=(
            P("dp", "seq", None),
            P(None, "dp", "seq", None, None),
            P(None, None, None, "dp"),
        ),
        out_specs=(P("dp", "seq", None), P("seq", None, None, "dp")),
        check_vma=False,
    )
```

```python
import jax
import jax.numpy as jnp
from jax import lax
from jax.experimental import pallas as pl
from jax.experimental.pallas import tpu as pltpu
from jax.sharding import PartitionSpec as P

F32 = jnp.float32
BF16 = jnp.bfloat16
TOP = 2.0**30
MESH = pl.DeviceIdType.MESH


def encode(x):
    square = x * x
    return (square * x * jnp.abs(x)).astype(BF16)


def decode(y):
    y = y.astype(F32)
    root = jnp.sqrt(jnp.sqrt(jnp.abs(y)))
    return jnp.where(y < 0, -root, root)


def kernel(ndp, nseq, cot, enc, w, ig, wg, near, far, encs, recv, send, wv, igs, igr, xs, xr, pks, pkr, pkz,
           wsem, ss_cot, rs_cot, ss_enc, rs_enc, ss_z, rs_z, ss_ig, rs_ig, ss_pk, rs_pk, ss_pz, rs_pz):
    nz = nseq // 2
    _, lc, rows, el = cot.shape
    dl = enc.shape[2]
    feats = w.shape[1]
    tokens = rows * nseq * ndp
    me, seq = lax.axis_index("dp"), lax.axis_index("seq")
    y, z = seq % 2, seq // 2
    pair = me + 1 - 2 * (me % 2)
    across = me + 2 - 4 * (me // 2)
    dps = (me, pair, across, 3 - me)
    ypeer = z * 2 + 1 - y

    def dp_dev(k):
        return (dps[k], seq)

    y_dev = (me, ypeer)

    def z_dev(zz):
        return (me, zz * 2 + y)

    def rcopy(src, dst, s, r, dev):
        return pltpu.make_async_remote_copy(
            src_ref=src, dst_ref=dst, send_sem=s, recv_sem=r, device_id=dev, device_id_type=MESH
        )

    barrier = pltpu.get_barrier_semaphore()
    for k in (1, 2, 3):
        pl.semaphore_signal(barrier, inc=1, device_id=dp_dev(k), device_id_type=MESH)
    pl.semaphore_signal(barrier, inc=1, device_id=y_dev, device_id_type=MESH)

    @pl.loop(1, nz)
    def _(d):
        pl.semaphore_signal(barrier, inc=1, device_id=z_dev((z + d) % nz), device_id_type=MESH)

    pl.semaphore_wait(barrier, 4 + nz - 1)

    wcopy = pltpu.make_async_copy(w, wv, wsem)

    def enc_copy(slot, src, dev):
        return rcopy(src, encs.at[slot], ss_enc.at[slot], rs_enc.at[slot], dev)

    e_y = enc_copy(1, enc.at[1 - y], y_dev)
    e_own2 = enc_copy(4, enc.at[y], dp_dev(2))
    e_own1 = enc_copy(2, enc.at[y], dp_dev(1))
    e_far2 = enc_copy(5, encs.at[1], dp_dev(2))
    e_far1 = enc_copy(3, encs.at[1], dp_dev(1))
    e_on1 = enc_copy(6, encs.at[4], dp_dev(1))
    e_on1f = enc_copy(7, encs.at[5], dp_dev(1))

    def near_ref(c, k):
        return cot.at[me, c] if k == 0 else near.at[c, k - 1]

    def dp_copy(c, k):
        return rcopy(cot.at[dps[k], c], near.at[c, k - 1], ss_cot.at[c, k], rs_cot.at[c, k], dp_dev(k))

    def y_copy(c, k):
        return rcopy(near_ref(c, k), far.at[c, k], ss_cot.at[c, 4 + k], rs_cot.at[c, 4 + k], y_dev)

    e_y.start()
    e_own2.start()
    y_copy(0, 0).start()
    dp_copy(0, 1).start()
    dp_copy(0, 2).start()
    dp_copy(0, 3).start()
    e_own1.start()
    wcopy.start()

    def dp_start(c):
        if c < lc:
            for k in (2, 3, 1):
                dp_copy(c, k).start()

    def cot_peak(i, m):
        return jnp.maximum(m, jnp.max(jnp.abs(cot[i // lc, i % lc].astype(F32)), axis=0, keepdims=True))

    def enc_peak(i, m):
        return jnp.maximum(m, jnp.max(jnp.abs(enc[i // nz, i % nz].astype(F32)), axis=0, keepdims=True))

    mc = jnp.max(lax.fori_loop(0, ndp * lc, cot_peak, jnp.zeros((1, el), F32)), axis=1, keepdims=True)
    me_ = jnp.max(lax.fori_loop(0, 2 * nz, enc_peak, jnp.zeros((1, rows), F32)), axis=1, keepdims=True)
    upper = lax.broadcasted_iota(jnp.int32, (8, 128), 0) < 4
    tile = jnp.where(upper, jnp.broadcast_to(me_, (8, 128)), jnp.broadcast_to(mc, (8, 128)))

    def pk_copy(i, dev):
        return rcopy(pks.at[i], pkr.at[i], ss_pk.at[i], rs_pk.at[i], dev)

    def pk_stage(i):
        pk_copy(i, None if i < 0 else (dp_dev(1), dp_dev(2), y_dev)[i]).wait_recv()
        pks[i + 1] = jnp.maximum(pks[i], pkr[i])

    pks[0] = tile
    pk_copy(0, dp_dev(1)).start()

    dp_start(1)
    dp_copy(0, 1).wait_recv()
    y_copy(0, 1).start()
    pk_stage(0)
    pk_copy(1, dp_dev(2)).start()
    e_y.wait_recv()
    e_far2.start()
    e_far1.start()
    e_own2.wait_recv()
    e_on1.start()
    for k in (2, 3):
        dp_copy(0, k).wait_recv()
        y_copy(0, k).start()
    dp_start(2)
    pk_stage(1)
    pk_copy(2, y_dev).start()

    def forward(c):
        for k in range(4):
            if k:
                dp_copy(c, k).wait_recv()
            y_copy(c, k).start()
        dp_start(c + 2)

    def pz_copy(d):
        return rcopy(pks.at[3], pkz.at[d], ss_pz.at[d], rs_pz.at[d], z_dev((z + d) % nz))

    e_far2.wait_recv()
    e_on1f.start()
    forward(1)
    pk_stage(2)
    pkz[0] = pks[3]

    @pl.loop(1, nz)
    def _(d):
        pz_copy(d).start()

    e_own1.wait_recv()
    e_far1.wait_recv()
    e_on1.wait_recv()
    e_on1f.wait_recv()

    @pl.loop(1, nz)
    def _(d):
        pz_copy(d).wait_recv()

    def pz_max(d, m):
        return jnp.maximum(m, pkz[d])

    peak = jnp.maximum(lax.fori_loop(1, nz, pz_max, pkz[0]), 1e-30)
    peak_e, peak_c = peak[0:1, 0:1], peak[4:5, 0:1]
    up_e = (TOP / tokens) / peak_e
    up_c = 1.0 / peak_c
    norm = 1.0 / jnp.sqrt(jnp.full((1, 1), tokens, F32))
    down = peak_e * peak_c * (tokens / TOP) * norm

    def term(b, c):
        lhs = jnp.concatenate([enc[y, b]] + [encs[s, b] for s in range(1, 2 * ndp)], axis=1)
        pieces = []
        for k in range(ndp):
            pieces += [cot[me, c] if k == 0 else near[c, k - 1], far[c, k]]
        rhs = jnp.concatenate(pieces, axis=0)
        t = jnp.dot(lhs, rhs, preferred_element_type=F32)
        return t * up_e * up_c

    lower = z < nz // 2
    way = jnp.where(lower, 0, 1)
    m = jnp.where(lower, z, nz - 1 - z)

    def z_copy(c, d, j, slot):
        return rcopy(send.at[c, slot], recv.at[c, d, j], ss_z.at[c, slot], rs_z.at[c, d, j], z_dev(z + 1 - 2 * d))

    def move(c, d, j, slot, has_prev):
        block = jnp.where(d == 0, nz - 1 - j, j)

        @pl.when(has_prev)
        def _():
            z_copy(c, d, j, slot).wait_recv()
            send[c, slot] = encode(term(block, c) + decode(recv[c, d, j]))

        @pl.when(jnp.logical_not(has_prev))
        def _():
            send[c, slot] = encode(term(block, c))


        z_copy(c, d, j, slot).start()

    def first(c):
        @pl.loop(0, nz - 1 - m)
        def _(j):
            move(c, way, j, j, m > 0)

    def second(c):
        @pl.loop(0, m)
        def _(j):
            move(c, 1 - way, j, nz - 1 - m + j, True)

    def finish(c):
        wg[c] = term(z, c)
        for d in range(2):
            j = nz - 1 - z if d == 0 else z

            @pl.when(z > 0 if d == 0 else z < nz - 1)
            def _():
                z_copy(c, d, j, 0).wait_recv()
                wg[c] = wg[c] + decode(recv[c, d, j])

        wg[c] = wg[c] * down

    step_f = 512 if feats % 512 == 0 else feats

    def partial(ka, kb, put):
        @pl.loop(0, feats // step_f)
        def _(i):
            cols = pl.ds(pl.multiple_of(i * step_f, step_f), step_f)
            acc = jnp.zeros((2 * rows, step_f), F32)
            for c in range(lc):
                lhs = jnp.concatenate([near_ref(c, ka)[...], near_ref(c, kb)[...]], axis=0)
                acc = acc + lax.dot_general(
                    lhs, wv[c, cols, :], (((1,), (1,)), ((), ())), preferred_element_type=F32
                )
            put(cols, acc)

    def ig_copy(i):
        return rcopy(igs.at[i], igr.at[i], ss_ig.at[i], rs_ig.at[i], dp_dev(1))

    x_copy = rcopy(xs.at[0], xr, ss_ig.at[2], rs_ig.at[2], dp_dev(2))

    def put_pair(cols, acc):
        igs[0, :, cols] = acc[:rows]
        igs[1, :, cols] = acc[rows:]

    def put_own(cols, acc):
        xs[0, :, cols] = acc[:rows] + igr[0, :, cols]
        xs[1, :, cols] = acc[rows:] + igr[1, :, cols]

    for c in range(lc):
        for k in range(4):
            y_copy(c, k).wait_recv()
        first(c)
        if c + 2 < lc:
            forward(c + 2)
        if c == lc - 3:
            wcopy.wait()
            partial(3, 1, put_pair)
            ig_copy(0).start()
            ig_copy(1).start()
        if c > 0:
            second(c - 1)
        if c == lc - 2:
            ig_copy(0).wait_recv()
            ig_copy(1).wait_recv()
            partial(2, 0, put_own)
            x_copy.start()
        if c > 1:
            finish(c - 2)
    finish(lc - 2)
    second(lc - 1)
    x_copy.wait_recv()
    ig[...] = (xs[1] + xr[...]).astype(BF16)
    finish(lc - 1)

    for c in range(lc):
        for k in range(4):
            if k:
                dp_copy(c, k).wait_send()
            y_copy(c, k).wait_send()

        @pl.loop(0, nz - 1)
        def _(j):
            z_copy(c, 0, 0, j).wait_send()

    for e in (e_y, e_own1, e_own2, e_far1, e_far2, e_on1, e_on1f, ig_copy(0), ig_copy(1), x_copy):
        e.wait_send()
    for i in range(3):
        pk_copy(i, y_dev).wait_send()

    @pl.loop(1, nz)
    def _(d):
        pz_copy(d).wait_send()


def local(encoded, cotangents, weights):
    ndp, nseq = lax.axis_size("dp"), lax.axis_size("seq")
    nz = nseq // 2
    layers, _, rows, parts, units = cotangents.shape
    feats = encoded.shape[2]
    dl = feats // nseq
    el = units // ndp
    lc = layers * parts
    cot = cotangents[:, 0].reshape(layers, rows, parts, ndp, el)
    cot = cot.transpose(3, 0, 2, 1, 4).reshape(ndp, lc, rows, el)
    enc = encoded[0].reshape(rows, nz, 2, dl).transpose(2, 1, 3, 0)
    w = weights.reshape(lc, feats, el)
    dma = pltpu.SemaphoreType.DMA
    ig, wg = pl.pallas_call(
        lambda *refs: kernel(ndp, nseq, *refs),
        out_shape=(
            jax.ShapeDtypeStruct((rows, feats), BF16),
            jax.ShapeDtypeStruct((lc, dl, el), F32),
        ),
        in_specs=[
            pl.BlockSpec(memory_space=pltpu.VMEM),
            pl.BlockSpec(memory_space=pltpu.VMEM),
            pl.BlockSpec(memory_space=pl.ANY),
        ],
        out_specs=(pl.BlockSpec(memory_space=pltpu.VMEM), pl.BlockSpec(memory_space=pltpu.VMEM)),
        scratch_shapes=[
            pltpu.VMEM((lc, ndp - 1, rows, el), BF16),
            pltpu.VMEM((lc, ndp, rows, el), BF16),
            pltpu.VMEM((2 * ndp, nz, dl, rows), BF16),
            pltpu.VMEM((lc, 2, nz - 1, dl, el), BF16),
            pltpu.VMEM((lc, nz - 1, dl, el), BF16),
            pltpu.VMEM((lc, feats, el), BF16),
            pltpu.VMEM((2, rows, feats), F32),
            pltpu.VMEM((2, rows, feats), F32),
            pltpu.VMEM((2, rows, feats), F32),
            pltpu.VMEM((rows, feats), F32),
            pltpu.VMEM((4, 8, 128), F32),
            pltpu.VMEM((3, 8, 128), F32),
            pltpu.VMEM((nz, 8, 128), F32),
            dma,
            dma((lc, 8)),
            dma((lc, 8)),
            dma((8,)),
            dma((8,)),
            dma((lc, nz - 1)),
            dma((lc, 2, nz - 1)),
            dma((3,)),
            dma((3,)),
            dma((3,)),
            dma((3,)),
            dma((nz,)),
            dma((nz,)),
        ],
        compiler_params=pltpu.CompilerParams(
            collective_id=0, has_side_effects=True, vmem_limit_bytes=56 * 2**20
        ),
    )(cot, enc, w)
    weight_grad = wg.reshape(layers, parts, dl, el).transpose(2, 0, 1, 3)
    return (ig[None], weight_grad)


def solution(mesh):
    return jax.shard_map(
        local,
        mesh=mesh,
        in_specs=(
            P("dp", "seq", None),
            P(None, "dp", "seq", None, None),
            P(None, None, None, "dp"),
        ),
        out_specs=(P("dp", "seq", None), P("seq", None, None, "dp")),
        check_vma=False,
    )
```

```python
import jax
import jax.numpy as jnp
from jax import lax
from jax.experimental import pallas as pl
from jax.experimental.pallas import tpu as pltpu
from jax.sharding import PartitionSpec as P

F32 = jnp.float32
BF16 = jnp.bfloat16
TOP = 2.0**30
MESH = pl.DeviceIdType.MESH


def encode(x):
    square = x * x
    return (square * x * jnp.abs(x)).astype(BF16)


def decode(y):
    y = y.astype(F32)
    root = jnp.sqrt(jnp.sqrt(jnp.abs(y)))
    return jnp.where(y < 0, -root, root)


def kernel(ndp, nseq, cot, enc, w, ig, wg, near, far, encs, recv, send, wv, igs, igr, xs, xr, pks, pkr, pkz,
           wsem, ss_cot, rs_cot, ss_enc, rs_enc, ss_z, rs_z, ss_ig, rs_ig, ss_pk, rs_pk, ss_pz, rs_pz):
    nz = nseq // 2
    lc, rows, units = cot.shape
    el = units // ndp
    dl = enc.shape[2]
    feats = w.shape[1]
    tokens = rows * nseq * ndp
    me, seq = lax.axis_index("dp"), lax.axis_index("seq")
    y, z = seq % 2, seq // 2
    pair = me + 1 - 2 * (me % 2)
    across = me + 2 - 4 * (me // 2)
    dps = (me, pair, across, 3 - me)
    ypeer = z * 2 + 1 - y

    def dp_dev(k):
        return (dps[k], seq)

    y_dev = (me, ypeer)

    def z_dev(zz):
        return (me, zz * 2 + y)

    def rcopy(src, dst, s, r, dev):
        return pltpu.make_async_remote_copy(
            src_ref=src, dst_ref=dst, send_sem=s, recv_sem=r, device_id=dev, device_id_type=MESH
        )

    barrier = pltpu.get_barrier_semaphore()
    for k in (1, 2, 3):
        pl.semaphore_signal(barrier, inc=1, device_id=dp_dev(k), device_id_type=MESH)
    pl.semaphore_signal(barrier, inc=1, device_id=y_dev, device_id_type=MESH)

    @pl.loop(1, nz)
    def _(d):
        pl.semaphore_signal(barrier, inc=1, device_id=z_dev((z + d) % nz), device_id_type=MESH)

    pl.semaphore_wait(barrier, 4 + nz - 1)

    wcopy = pltpu.make_async_copy(w, wv, wsem)

    def enc_copy(slot, src, dev):
        return rcopy(src, encs.at[slot], ss_enc.at[slot], rs_enc.at[slot], dev)

    e_y = enc_copy(1, enc.at[1 - y], y_dev)
    e_own2 = enc_copy(4, enc.at[y], dp_dev(2))
    e_own1 = enc_copy(2, enc.at[y], dp_dev(1))
    e_far2 = enc_copy(5, encs.at[1], dp_dev(2))
    e_far1 = enc_copy(3, encs.at[1], dp_dev(1))
    e_on1 = enc_copy(6, encs.at[4], dp_dev(1))
    e_on1f = enc_copy(7, encs.at[5], dp_dev(1))

    def head(i):
        return pl.ds(pl.multiple_of(i * el, el), el)

    def near_ref(c, k):
        return cot.at[c, :, head(me)] if k == 0 else near.at[c, k - 1]

    def dp_copy(c, k):
        return rcopy(cot.at[c, :, head(dps[k])], near.at[c, k - 1], ss_cot.at[c, k], rs_cot.at[c, k], dp_dev(k))

    def y_copy(c, k):
        return rcopy(near_ref(c, k), far.at[c, k], ss_cot.at[c, 4 + k], rs_cot.at[c, 4 + k], y_dev)

    e_y.start()
    e_own2.start()
    y_copy(0, 0).start()
    dp_copy(0, 1).start()
    dp_copy(0, 2).start()
    dp_copy(0, 3).start()
    e_own1.start()
    wcopy.start()

    def dp_start(c):
        if c < lc:
            for k in (2, 3, 1):
                dp_copy(c, k).start()

    def cot_peak(i, m):
        return jnp.maximum(m, jnp.max(jnp.abs(cot[i // ndp, :, head(i % ndp)].astype(F32)), axis=0, keepdims=True))

    def enc_peak(i, m):
        return jnp.maximum(m, jnp.max(jnp.abs(enc[i // nz, i % nz].astype(F32)), axis=0, keepdims=True))

    mc = jnp.max(lax.fori_loop(0, ndp * lc, cot_peak, jnp.zeros((1, el), F32)), axis=1, keepdims=True)
    me_ = jnp.max(lax.fori_loop(0, 2 * nz, enc_peak, jnp.zeros((1, rows), F32)), axis=1, keepdims=True)
    upper = lax.broadcasted_iota(jnp.int32, (8, 128), 0) < 4
    tile = jnp.where(upper, jnp.broadcast_to(me_, (8, 128)), jnp.broadcast_to(mc, (8, 128)))

    def pk_copy(i, dev):
        return rcopy(pks.at[i], pkr.at[i], ss_pk.at[i], rs_pk.at[i], dev)

    def pk_stage(i):
        pk_copy(i, None if i < 0 else (dp_dev(1), dp_dev(2), y_dev)[i]).wait_recv()
        pks[i + 1] = jnp.maximum(pks[i], pkr[i])

    pks[0] = tile
    pk_copy(0, dp_dev(1)).start()

    dp_start(1)
    dp_copy(0, 1).wait_recv()
    y_copy(0, 1).start()
    pk_stage(0)
    pk_copy(1, dp_dev(2)).start()
    e_y.wait_recv()
    e_far2.start()
    e_far1.start()
    e_own2.wait_recv()
    e_on1.start()
    for k in (2, 3):
        dp_copy(0, k).wait_recv()
        y_copy(0, k).start()
    dp_start(2)
    pk_stage(1)
    pk_copy(2, y_dev).start()

    def forward(c):
        for k in range(4):
            if k:
                dp_copy(c, k).wait_recv()
            y_copy(c, k).start()
        dp_start(c + 2)

    def pz_copy(d):
        return rcopy(pks.at[3], pkz.at[d], ss_pz.at[d], rs_pz.at[d], z_dev((z + d) % nz))

    e_far2.wait_recv()
    e_on1f.start()
    forward(1)
    pk_stage(2)
    pkz[0] = pks[3]

    @pl.loop(1, nz)
    def _(d):
        pz_copy(d).start()

    e_own1.wait_recv()
    e_far1.wait_recv()
    e_on1.wait_recv()
    e_on1f.wait_recv()

    @pl.loop(1, nz)
    def _(d):
        pz_copy(d).wait_recv()

    def pz_max(d, m):
        return jnp.maximum(m, pkz[d])

    peak = jnp.maximum(lax.fori_loop(1, nz, pz_max, pkz[0]), 1e-30)
    peak_e, peak_c = peak[0:1, 0:1], peak[4:5, 0:1]
    up_e = (TOP / tokens) / peak_e
    up_c = 1.0 / peak_c
    norm = 1.0 / jnp.sqrt(jnp.full((1, 1), tokens, F32))
    down = peak_e * peak_c * (tokens / TOP) * norm

    def term(b, c):
        lhs = jnp.concatenate([enc[y, b]] + [encs[s, b] for s in range(1, 2 * ndp)], axis=1)
        pieces = []
        for k in range(ndp):
            pieces += [cot[c, :, head(me)] if k == 0 else near[c, k - 1], far[c, k]]
        rhs = jnp.concatenate(pieces, axis=0)
        t = jnp.dot(lhs, rhs, preferred_element_type=F32)
        return t * up_e * up_c

    lower = z < nz // 2
    way = jnp.where(lower, 0, 1)
    m = jnp.where(lower, z, nz - 1 - z)

    def z_copy(c, d, j, slot):
        return rcopy(send.at[c, slot], recv.at[c, d, j], ss_z.at[c, slot], rs_z.at[c, d, j], z_dev(z + 1 - 2 * d))

    def move(c, d, j, slot, has_prev):
        block = jnp.where(d == 0, nz - 1 - j, j)

        @pl.when(has_prev)
        def _():
            z_copy(c, d, j, slot).wait_recv()
            send[c, slot] = encode(term(block, c) + decode(recv[c, d, j]))

        @pl.when(jnp.logical_not(has_prev))
        def _():
            send[c, slot] = encode(term(block, c))


        z_copy(c, d, j, slot).start()

    def first(c):
        @pl.loop(0, nz - 1 - m)
        def _(j):
            move(c, way, j, j, m > 0)

    def second(c):
        @pl.loop(0, m)
        def _(j):
            move(c, 1 - way, j, nz - 1 - m + j, True)

    def finish(c):
        wg[c] = term(z, c)
        for d in range(2):
            j = nz - 1 - z if d == 0 else z

            @pl.when(z > 0 if d == 0 else z < nz - 1)
            def _():
                z_copy(c, d, j, 0).wait_recv()
                wg[c] = wg[c] + decode(recv[c, d, j])

        wg[c] = wg[c] * down

    step_f = 512 if feats % 512 == 0 else feats

    def partial(ka, kb, put):
        @pl.loop(0, feats // step_f)
        def _(i):
            cols = pl.ds(pl.multiple_of(i * step_f, step_f), step_f)
            acc = jnp.zeros((2 * rows, step_f), F32)
            for c in range(lc):
                lhs = jnp.concatenate([near_ref(c, ka)[...], near_ref(c, kb)[...]], axis=0)
                acc = acc + lax.dot_general(
                    lhs, wv[c, cols, :], (((1,), (1,)), ((), ())), preferred_element_type=F32
                )
            put(cols, acc)

    def ig_copy(i):
        return rcopy(igs.at[i], igr.at[i], ss_ig.at[i], rs_ig.at[i], dp_dev(1))

    x_copy = rcopy(xs.at[0], xr, ss_ig.at[2], rs_ig.at[2], dp_dev(2))

    def put_pair(cols, acc):
        igs[0, :, cols] = acc[:rows]
        igs[1, :, cols] = acc[rows:]

    def put_own(cols, acc):
        xs[0, :, cols] = acc[:rows] + igr[0, :, cols]
        xs[1, :, cols] = acc[rows:] + igr[1, :, cols]

    for c in range(lc):
        for k in range(4):
            y_copy(c, k).wait_recv()
        first(c)
        if c + 2 < lc:
            forward(c + 2)
        if c == lc - 3:
            wcopy.wait()
            partial(3, 1, put_pair)
            ig_copy(0).start()
            ig_copy(1).start()
        if c > 0:
            second(c - 1)
        if c == lc - 2:
            ig_copy(0).wait_recv()
            ig_copy(1).wait_recv()
            partial(2, 0, put_own)
            x_copy.start()
        if c > 1:
            finish(c - 2)
    second(lc - 1)
    finish(lc - 2)
    x_copy.wait_recv()
    ig[...] = (xs[1] + xr[...]).astype(BF16)
    finish(lc - 1)

    for c in range(lc):
        for k in range(4):
            if k:
                dp_copy(c, k).wait_send()
            y_copy(c, k).wait_send()

        @pl.loop(0, nz - 1)
        def _(j):
            z_copy(c, 0, 0, j).wait_send()

    for e in (e_y, e_own1, e_own2, e_far1, e_far2, e_on1, e_on1f, ig_copy(0), ig_copy(1), x_copy):
        e.wait_send()
    for i in range(3):
        pk_copy(i, y_dev).wait_send()

    @pl.loop(1, nz)
    def _(d):
        pz_copy(d).wait_send()


def local(encoded, cotangents, weights):
    ndp, nseq = lax.axis_size("dp"), lax.axis_size("seq")
    nz = nseq // 2
    layers, _, rows, parts, units = cotangents.shape
    feats = encoded.shape[2]
    dl = feats // nseq
    el = units // ndp
    lc = layers * parts
    cot = cotangents[:, 0].transpose(0, 2, 1, 3).reshape(lc, rows, units)
    enc = encoded[0].reshape(rows, nz, 2, dl).transpose(2, 1, 3, 0)
    w = weights.reshape(lc, feats, el)
    dma = pltpu.SemaphoreType.DMA
    ig, wg = pl.pallas_call(
        lambda *refs: kernel(ndp, nseq, *refs),
        out_shape=(
            jax.ShapeDtypeStruct((rows, feats), BF16),
            jax.ShapeDtypeStruct((lc, dl, el), F32),
        ),
        in_specs=[
            pl.BlockSpec(memory_space=pltpu.VMEM),
            pl.BlockSpec(memory_space=pltpu.VMEM),
            pl.BlockSpec(memory_space=pl.ANY),
        ],
        out_specs=(pl.BlockSpec(memory_space=pltpu.VMEM), pl.BlockSpec(memory_space=pltpu.VMEM)),
        scratch_shapes=[
            pltpu.VMEM((lc, ndp - 1, rows, el), BF16),
            pltpu.VMEM((lc, ndp, rows, el), BF16),
            pltpu.VMEM((2 * ndp, nz, dl, rows), BF16),
            pltpu.VMEM((lc, 2, nz - 1, dl, el), BF16),
            pltpu.VMEM((lc, nz - 1, dl, el), BF16),
            pltpu.VMEM((lc, feats, el), BF16),
            pltpu.VMEM((2, rows, feats), F32),
            pltpu.VMEM((2, rows, feats), F32),
            pltpu.VMEM((2, rows, feats), F32),
            pltpu.VMEM((rows, feats), F32),
            pltpu.VMEM((4, 8, 128), F32),
            pltpu.VMEM((3, 8, 128), F32),
            pltpu.VMEM((nz, 8, 128), F32),
            dma,
            dma((lc, 8)),
            dma((lc, 8)),
            dma((8,)),
            dma((8,)),
            dma((lc, nz - 1)),
            dma((lc, 2, nz - 1)),
            dma((3,)),
            dma((3,)),
            dma((3,)),
            dma((3,)),
            dma((nz,)),
            dma((nz,)),
        ],
        compiler_params=pltpu.CompilerParams(
            collective_id=0, has_side_effects=True, vmem_limit_bytes=56 * 2**20
        ),
    )(cot, enc, w)
    weight_grad = wg.reshape(layers, parts, dl, el).transpose(2, 0, 1, 3)
    return (ig[None], weight_grad)


def solution(mesh):
    return jax.shard_map(
        local,
        mesh=mesh,
        in_specs=(
            P("dp", "seq", None),
            P(None, "dp", "seq", None, None),
            P(None, None, None, "dp"),
        ),
        out_specs=(P("dp", "seq", None), P("seq", None, None, "dp")),
        check_vma=False,
    )
```
